32 devices in a mesh: groups: 1, expert: 8 (over z, y), dp: 4 (over x, core).
Axes of the slice: x: 2, y: 2, z: 4, core: 2. Of those that a mesh axis runs over, the one named last changes fastest.
Arguments:
- tokens: bfloat16 [4096, 2048], P(('groups', 'expert', 'dp')), may hold values from -6 to 6
- expert_ids: int32 [4096, 8], P(('groups', 'expert', 'dp')), may hold values from 0 to 15, all different within a row; in each aligned block of 128 rows (0 to 127, 128 to 255, ...) at most 96 rows name the same one
- gate_scores: float32 [4096, 8], P(('groups', 'expert', 'dp')), may hold values from 0.05 to 1
- w_gate: bfloat16 [32, 2048, 192], P(('expert', 'dp')), may hold values from -0.125 to 0.125
- w_up: bfloat16 [32, 2048, 192], P(('expert', 'dp')), may hold values from -0.125 to 0.125
- w_down: bfloat16 [32, 192, 2048], P(('expert', 'dp')), may hold values from -0.3125 to 0.3125
- projector: bfloat16 [2048, 1536], P(None, 'dp'), may hold values from -0.125 to 0.125
- student: bfloat16 [4096, 1536], P(('groups', 'expert'), 'dp'), may hold values from -6 to 6
- target_mask: int32 [4096], P(('groups', 'expert')), may hold values 0 or 1
Outputs:
- projected: bfloat16 [4096, 1536], P(('groups', 'expert'), 'dp')
- proj_grad: float32 [2048, 1536], P(('groups', 'expert'), 'dp')
The draws below stay inside these ranges and needn't reach their ends.
Inputs may be any that keep to these rules, and one draw needn't show every extreme that they name: `expert_ids`: each token names 8 different experts. Within each aligned block of 128 tokens (the tokens of one device) no expert is named by more than 96 tokens, and in every draw some expert is named by exactly 96 tokens of some block.
All inputs are finite; a program needn't handle non-finite values. No bound on the sum of `target_mask` on one device may be relied on, other than what follows from the above.
Results may differ from the reference program's by a relative error of at most 0.012.
Values may be sent and summed in bfloat16 or wider, within the bound.
A program may use at most 128 MiB of HBM per device.

```python
import math
import jax
import jax.numpy as jnp
import numpy as np
from jax import lax

D = 2048
TOPK = 8
SD = 1536
FF = 384
TOK_DEV = 128
HALF = 192
EXPERTS = 16
TOKENS = 4096
CAP = 96


def touch_ends(result, rng, low, top_value):
    longest = result.shape.index(max(result.shape))
    spots = []
    for shift in (0, 1):
        where = [jax.random.randint(jax.random.fold_in(rng, axis), (), 0, length) for axis, length in enumerate(result.shape)]
        where[longest] = (where[longest] + shift) % result.shape[longest]
        spots.append(tuple(where))
    return result.at[spots[0]].set(low).at[spots[1]].set(top_value)


def steps_of(stream_key, extent, shards, smallest, largest):
    loudness, own = 1.0, jax.random.fold_in(stream_key, 6)
    for dim, parts in shards:
        draws = jnp.exp(jax.random.uniform(jax.random.fold_in(own, dim), (parts,), jnp.float32, smallest / len(shards), largest / len(shards)))
        loudness = loudness * jnp.repeat(draws, extent[dim] // parts).reshape([-1 if axis == dim else 1 for axis in range(len(extent))])
    return loudness


def assign_block(own_key, own, number, rows, amount, top, bound, lean):
    ranking = jax.random.permutation(own_key, amount)
    crowded, usual = portions_of(amount, rows * top, bound, lean, True), portions_of(amount, rows * top, bound, lean, False)
    places = jnp.arange(amount)

    def named(sizes, turn):
        used = int((sizes > 0).sum())
        fixed = max(1, used // 4)
        passed = fixed + (places - fixed + turn * (used - fixed)) % max(1, amount - fixed)
        return jnp.zeros((amount,), jnp.int32).at[ranking[jnp.where(places < fixed, places, passed)]].set(jnp.asarray(sizes, jnp.int32))

    sizes = jnp.where(number % 4 == 0, named(crowded, number // 4), named(usual, number - number // 4 - 1))
    mixed = jax.random.permutation(jax.random.fold_in(own, 3), amount)
    source_of, sink = mixed[0:amount // 2 * 2:2], mixed[1:amount // 2 * 2:2]
    margin = jnp.minimum(sizes[source_of] - 1, bound - sizes[sink]) // 2
    margin = jnp.where((source_of == ranking[0]) | (sink == ranking[0]) | (sizes[sink] == 0), 0, jnp.maximum(margin, 0))
    passed = jax.random.randint(jax.random.fold_in(own, 4), (amount // 2,), 0, 1 << 20) % (margin + 1)
    sizes = sizes.at[source_of].add(-passed).at[sink].add(passed)
    members = jnp.searchsorted(jnp.cumsum(sizes), jnp.arange(rows * top), side="right").astype(jnp.int32)
    grid = members.reshape(top, rows).T
    grid = grid[jax.random.permutation(jax.random.fold_in(own, 1), rows)]
    turn = jax.random.randint(jax.random.fold_in(own, 2), (rows, 1), 0, top)
    return jnp.take_along_axis(grid, (jnp.arange(top)[None, :] + turn) % top, axis=1)


def portions_of(amount, total, most, lean, full):
    weights = [(1 << 20) // math.isqrt(grade ** lean) + 1 for grade in range(1, amount + 1)]
    largest = most if full else min(most, max(-(-total // amount), total * weights[0] // sum(weights)))
    least = 1 if total - largest >= amount - 1 else 0
    holding, surplus = [largest] + [least] * (amount - 1), total - largest - least * (amount - 1)
    while surplus > 0:
        free = [i for i in range(1, amount) if holding[i] < largest] or [i for i in range(1, amount) if holding[i] < most]
        whole, budget = sum([weights[i] for i in free]), surplus
        for i in free:
            addition = min(most - holding[i], max(1, budget * weights[i] // whole), surplus)
            holding[i] = holding[i] + addition
            surplus = surplus - addition
    return np.array(holding)


def normal_values(rng, shape, scale, bound, shards=(), kind=jnp.bfloat16):
    result = jax.random.normal(rng, shape, jnp.float32) * scale
    if len(shards) > 0:
        result = steps_of(rng, shape, shards, -0.22, 0.18) * result
    return jnp.clip(result, min=-bound, max=bound).astype(kind)


def setup_inputs(seed: int = 0, part: int = 0) -> dict:
    splits = jax.random.split(jax.random.key(seed), 10)
    part_keys = jax.random.split(jax.random.fold_in(splits[9], part), 10)
    tokens = normal_values(part_keys[0], (TOKENS, D), 1.0, 6.0, ((0, 32),))
    expert_ids_keys = jax.random.split(jax.random.fold_in(part_keys[1], 1), TOKENS // TOK_DEV)
    expert_ids_turns = jax.random.permutation(jax.random.fold_in(part_keys[1], 3), TOKENS // TOK_DEV)
    expert_ids = jax.vmap(lambda own, number: assign_block(jax.random.fold_in(part_keys[1], 2), own, number, TOK_DEV, EXPERTS, TOPK, CAP, 2))(expert_ids_keys, expert_ids_turns).reshape((TOKENS, TOPK))
    gate_scores = jnp.clip(jnp.exp(math.log(1.0) - 2.9957323 * jax.random.uniform(part_keys[2], (TOKENS, TOPK), jnp.float32) ** steps_of(part_keys[2], (TOKENS, TOPK), ((0, 32),), -0.2, 0.2)), 0.05, 1.0)
    w_gate = normal_values(splits[3], (2 * EXPERTS, D, HALF), D ** -0.5, 0.125, ((0, 32),))
    w_up = normal_values(splits[4], (2 * EXPERTS, D, HALF), D ** -0.5, 0.125, ((0, 32),))
    w_down = normal_values(splits[5], (2 * EXPERTS, HALF, D), FF ** -0.5, 0.3125, ((0, 32),))
    projector = normal_values(splits[6], (D, SD), D ** -0.5, 0.125, ((1, 4),))
    student = normal_values(part_keys[7], (TOKENS, SD), 1.0, 6.0, ((0, 8), (1, 4)))
    target_mask = touch_ends((jax.random.randint(part_keys[8], (TOKENS,), 0, 4) < 3).astype(jnp.int32), jax.random.fold_in(part_keys[8], 1), 0, 1)
    return dict(tokens=tokens, expert_ids=expert_ids, gate_scores=gate_scores, w_gate=w_gate, w_up=w_up, w_down=w_down, projector=projector, student=student, target_mask=target_mask)


def reference(tokens, expert_ids, gate_scores, w_gate, w_up, w_down, projector, student, target_mask):
    blocks = TOKENS // TOK_DEV
    naming = (expert_ids[:, :, None] == jnp.arange(EXPERTS, dtype=jnp.int32)[None, None, :]).astype(jnp.int32)
    expert_hits = lax.optimization_barrier(jnp.sum(naming, axis=1)).reshape(blocks, TOK_DEV, EXPERTS)
    earlier = (jnp.cumsum(expert_hits, axis=1) - expert_hits).reshape(TOKENS, EXPERTS)
    slot_index = lax.optimization_barrier(jnp.sum(naming * earlier[:, None, :], axis=2))
    token_block = (jnp.arange(TOKENS, dtype=jnp.int32) // TOK_DEV)[:, None]
    position = (token_block * CAP + slot_index).astype(jnp.int32)
    norm_gates = gate_scores / lax.optimization_barrier(jnp.sum(gate_scores, axis=1, keepdims=True))
    token_iota = jnp.broadcast_to(jnp.arange(TOKENS, dtype=jnp.int32)[:, None], (TOKENS, TOPK))
    table = jnp.full((EXPERTS, blocks * CAP), TOKENS, jnp.int32).at[expert_ids, position].set(token_iota)
    weight_table = jnp.zeros((EXPERTS, blocks * CAP), jnp.float32).at[expert_ids, position].set(norm_gates)
    padded = jnp.concatenate([tokens, jnp.zeros((1, D), tokens.dtype)], axis=0)
    gate_pairs = w_gate.reshape(EXPERTS, 2, D, HALF)
    up_pairs = w_up.reshape(EXPERTS, 2, D, HALF)
    down_full = w_down.reshape(EXPERTS, 2 * HALF, D)

    def expert_step(summed, expert_index):
        gathered = padded[table[expert_index]]
        gate_pair = gate_pairs[expert_index]
        up_pair = up_pairs[expert_index]
        gate_full = jnp.concatenate([gate_pair[0], gate_pair[1]], axis=1)
        up_full = jnp.concatenate([up_pair[0], up_pair[1]], axis=1)
        gate_pre = jnp.dot(gathered, gate_full, preferred_element_type=jnp.float32)
        up_pre = jnp.dot(gathered, up_full, preferred_element_type=jnp.float32)
        hidden = (jax.nn.silu(gate_pre) * up_pre).astype(jnp.bfloat16)
        expert_out = jnp.dot(hidden, down_full[expert_index], preferred_element_type=jnp.float32).astype(jnp.bfloat16)
        summed = summed.at[table[expert_index]].add(weight_table[expert_index][:, None] * expert_out.astype(jnp.float32))
        return (summed, None)
    summed, unused = lax.scan(expert_step, jnp.zeros((TOKENS + 1, D), jnp.float32), jnp.arange(EXPERTS, dtype=jnp.int32))
    teacher_out = summed[:TOKENS].astype(jnp.bfloat16)
    proj = jnp.dot(teacher_out, projector, preferred_element_type=jnp.float32)
    projected = proj.astype(jnp.bfloat16)
    error = (target_mask.astype(jnp.float32)[:, None] * (proj - student.astype(jnp.float32))).astype(jnp.bfloat16)
    proj_grad = jnp.dot(teacher_out.T, error, preferred_element_type=jnp.float32) * (1.0 / math.sqrt(TOKENS))
    return (projected, proj_grad)
```

```python
import math

import jax
import jax.numpy as jnp
from jax import lax
from jax.sharding import PartitionSpec as P


def from_partner(block, axis, apart):
    count = lax.axis_size(axis)
    route = []
    for low in range(count):
        high = low | 1 << apart
        if high != low and high < count:
            route += [(low, high), (high, low)]
    return lax.ppermute(block, axis, route)


def half_hidden(slot_rows, gate_half, up_half):
    gate_pre = jnp.dot(slot_rows, gate_half, preferred_element_type=jnp.float32)
    up_pre = jnp.dot(slot_rows, up_half, preferred_element_type=jnp.float32)
    return (jax.nn.silu(gate_pre) * up_pre).astype(jnp.bfloat16)


def routed_body(tokens, expert_ids, gate_scores, w_gate, w_up, w_down, projector, student, target_mask):
    tok_count = tokens.shape[0]
    model_width = tokens.shape[1]
    top_count = expert_ids.shape[1]
    expert_axis = lax.axis_size("expert")
    data_axis = lax.axis_size("dp")
    expert_total = expert_axis * data_axis // 2
    capacity = min(
        tok_count, 2 * ((3 * tok_count * top_count + 4 * expert_total - 1) // (4 * expert_total))
    )
    half_cap = capacity // 2
    slot_total = expert_total * capacity
    expert_iota = jnp.arange(expert_total, dtype=jnp.int32)
    naming = (expert_ids[:, :, None] == expert_iota[None, None, :]).astype(jnp.int32)
    expert_hits = jnp.sum(naming, axis=1)
    earlier = jnp.cumsum(expert_hits, axis=0) - expert_hits
    slot_index = jnp.sum(naming * earlier[:, None, :], axis=2)
    position = expert_ids * capacity + slot_index
    token_iota = jnp.broadcast_to(
        jnp.arange(tok_count, dtype=jnp.int32)[:, None], (tok_count, top_count)
    )
    slot_table = (
        jnp.full((slot_total,), tok_count, jnp.int32)
        .at[position.reshape(-1)]
        .set(token_iota.reshape(-1))
    )
    padded_tokens = jnp.concatenate([tokens, jnp.zeros((1, model_width), tokens.dtype)], axis=0)
    send_rows = jnp.take(padded_tokens, slot_table, axis=0)
    send_rows = send_rows.reshape(expert_axis, data_axis, half_cap, model_width)
    arrived = lax.all_to_all(
        lax.all_to_all(send_rows, "expert", split_axis=0, concat_axis=0, tiled=True),
        "dp",
        split_axis=1,
        concat_axis=1,
        tiled=True,
    )
    slot_rows = arrived.reshape(slot_total, model_width)
    gate_mine = w_gate[0]
    up_mine = w_up[0]
    down_mine = w_down[0]
    gate_other, up_other, down_other = from_partner((gate_mine, up_mine, down_mine), "dp", 0)
    hidden_mine = half_hidden(slot_rows, gate_mine, up_mine)
    hidden_other = half_hidden(slot_rows, gate_other, up_other)
    expert_out = (
        jnp.dot(hidden_mine, down_mine, preferred_element_type=jnp.float32)
        + jnp.dot(hidden_other, down_other, preferred_element_type=jnp.float32)
    ).astype(jnp.bfloat16)
    came_back = lax.all_to_all(
        lax.all_to_all(
            expert_out.reshape(expert_axis, data_axis, half_cap, model_width),
            "expert",
            split_axis=0,
            concat_axis=0,
            tiled=True,
        ),
        "dp",
        split_axis=1,
        concat_axis=1,
        tiled=True,
    )
    returned = came_back.reshape(slot_total, model_width)
    norm_gates = gate_scores / jnp.sum(gate_scores, axis=1, keepdims=True)
    combined = jnp.zeros((tok_count, model_width), jnp.float32)
    for column in range(top_count):
        picked = jnp.take(returned, position[:, column], axis=0)
        combined = combined + norm_gates[:, column : column + 1] * picked.astype(jnp.float32)
    teacher_out = combined.astype(jnp.bfloat16)
    return finish(teacher_out, projector, student, target_mask)


def dense_body(tokens, expert_ids, gate_scores, w_gate, w_up, w_down, projector, student, target_mask):
    tok_count, model_width = tokens.shape
    expert_axis = lax.axis_size("expert")
    data_axis = lax.axis_size("dp")
    expert_total = expert_axis * data_axis // 2
    held = data_axis // 2
    norm_gates = gate_scores / jnp.sum(gate_scores, axis=1, keepdims=True)
    iota = jnp.arange(expert_total, dtype=jnp.int32)
    dense_gates = jnp.sum(
        jnp.where(expert_ids[:, :, None] == iota[None, None, :], norm_gates[:, :, None], 0.0), axis=1
    )
    all_tokens = lax.all_gather(tokens, "expert", axis=0, tiled=True)
    all_gates = lax.all_gather(dense_gates, "expert", axis=0, tiled=True)
    gate_all = lax.all_gather(w_gate, "dp", axis=0, tiled=True)
    up_all = lax.all_gather(w_up, "dp", axis=0, tiled=True)
    down_all = lax.all_gather(w_down, "dp", axis=0, tiled=True)
    mine = lax.axis_index("expert") * held
    summed = jnp.zeros((tok_count * expert_axis, model_width), jnp.float32)
    for local in range(held):
        out = jnp.zeros((tok_count * expert_axis, model_width), jnp.float32)
        for half in range(2):
            slab = 2 * local + half
            hidden = half_hidden(all_tokens, gate_all[slab], up_all[slab])
            out = out + jnp.dot(hidden, down_all[slab], preferred_element_type=jnp.float32)
        gate = lax.dynamic_slice_in_dim(all_gates, mine + local, 1, axis=1)
        summed = summed + gate * out.astype(jnp.bfloat16).astype(jnp.float32)
    teacher_out = lax.psum_scatter(
        summed.astype(jnp.bfloat16), "expert", scatter_dimension=0, tiled=True
    )
    return finish(teacher_out, projector, student, target_mask)


def finish(teacher_out, projector, student, target_mask):
    grad_scale = 1.0 / math.sqrt(teacher_out.shape[0] * lax.axis_size("expert") * lax.axis_size("dp"))
    mask_rows = target_mask.astype(jnp.float32)
    portion = lax.all_gather(teacher_out, "dp", axis=0, tiled=True)
    proj_part = jnp.dot(portion, projector, preferred_element_type=jnp.float32)
    target_part = student.astype(jnp.float32)
    error_part = (mask_rows[:, None] * (proj_part - target_part)).astype(jnp.bfloat16)
    grad_term = lax.dot_general(
        portion, error_part, (((0,), (0,)), ((), ())), preferred_element_type=jnp.float32
    )
    grad_part = (
        lax.psum_scatter(
            grad_term.astype(jnp.bfloat16), "expert", scatter_dimension=0, tiled=True
        ).astype(jnp.float32)
        * grad_scale
    )
    return (proj_part.astype(jnp.bfloat16), grad_part)


def solution(mesh):
    experts = mesh.shape["expert"] * mesh.shape["dp"] // 2
    body = dense_body if experts <= 32 else routed_body
    return jax.shard_map(
        body,
        mesh=mesh,
        in_specs=(
            P(("groups", "expert", "dp"), None),
            P(("groups", "expert", "dp"), None),
            P(("groups", "expert", "dp"), None),
            P(("expert", "dp"), None, None),
            P(("expert", "dp"), None, None),
            P(("expert", "dp"), None, None),
            P(None, "dp"),
            P(("groups", "expert"), "dp"),
            P(("groups", "expert")),
        ),
        out_specs=(P(("groups", "expert"), "dp"), P(("groups", "expert"), "dp")),
        check_vma=False,
    )
```

```python
import functools
import math

import jax
import jax.numpy as jnp
from jax import lax
from jax.experimental import pallas as pl
from jax.experimental.pallas import tpu as pltpu
from jax.sharding import PartitionSpec as P


def from_partner(block, axis, apart):
    count = lax.axis_size(axis)
    route = []
    for low in range(count):
        high = low | 1 << apart
        if high != low and high < count:
            route += [(low, high), (high, low)]
    return lax.ppermute(block, axis, route)


def half_hidden(slot_rows, gate_half, up_half):
    gate_pre = jnp.dot(slot_rows, gate_half, preferred_element_type=jnp.float32)
    up_pre = jnp.dot(slot_rows, up_half, preferred_element_type=jnp.float32)
    return (jax.nn.silu(gate_pre) * up_pre).astype(jnp.bfloat16)


def routed_body(tokens, expert_ids, gate_scores, w_gate, w_up, w_down, projector, student, target_mask):
    tok_count = tokens.shape[0]
    model_width = tokens.shape[1]
    top_count = expert_ids.shape[1]
    expert_axis = lax.axis_size("expert")
    data_axis = lax.axis_size("dp")
    expert_total = expert_axis * data_axis // 2
    capacity = min(
        tok_count, 2 * ((3 * tok_count * top_count + 4 * expert_total - 1) // (4 * expert_total))
    )
    half_cap = capacity // 2
    slot_total = expert_total * capacity
    expert_iota = jnp.arange(expert_total, dtype=jnp.int32)
    naming = (expert_ids[:, :, None] == expert_iota[None, None, :]).astype(jnp.int32)
    expert_hits = jnp.sum(naming, axis=1)
    earlier = jnp.cumsum(expert_hits, axis=0) - expert_hits
    slot_index = jnp.sum(naming * earlier[:, None, :], axis=2)
    position = expert_ids * capacity + slot_index
    token_iota = jnp.broadcast_to(
        jnp.arange(tok_count, dtype=jnp.int32)[:, None], (tok_count, top_count)
    )
    slot_table = (
        jnp.full((slot_total,), tok_count, jnp.int32)
        .at[position.reshape(-1)]
        .set(token_iota.reshape(-1))
    )
    padded_tokens = jnp.concatenate([tokens, jnp.zeros((1, model_width), tokens.dtype)], axis=0)
    send_rows = jnp.take(padded_tokens, slot_table, axis=0)
    send_rows = send_rows.reshape(expert_axis, data_axis, half_cap, model_width)
    arrived = lax.all_to_all(
        lax.all_to_all(send_rows, "expert", split_axis=0, concat_axis=0, tiled=True),
        "dp",
        split_axis=1,
        concat_axis=1,
        tiled=True,
    )
    slot_rows = arrived.reshape(slot_total, model_width)
    gate_mine = w_gate[0]
    up_mine = w_up[0]
    down_mine = w_down[0]
    gate_other, up_other, down_other = from_partner((gate_mine, up_mine, down_mine), "dp", 0)
    hidden_mine = half_hidden(slot_rows, gate_mine, up_mine)
    hidden_other = half_hidden(slot_rows, gate_other, up_other)
    expert_out = (
        jnp.dot(hidden_mine, down_mine, preferred_element_type=jnp.float32)
        + jnp.dot(hidden_other, down_other, preferred_element_type=jnp.float32)
    ).astype(jnp.bfloat16)
    came_back = lax.all_to_all(
        lax.all_to_all(
            expert_out.reshape(expert_axis, data_axis, half_cap, model_width),
            "expert",
            split_axis=0,
            concat_axis=0,
            tiled=True,
        ),
        "dp",
        split_axis=1,
        concat_axis=1,
        tiled=True,
    )
    returned = came_back.reshape(slot_total, model_width)
    norm_gates = gate_scores / jnp.sum(gate_scores, axis=1, keepdims=True)
    combined = jnp.zeros((tok_count, model_width), jnp.float32)
    for column in range(top_count):
        picked = jnp.take(returned, position[:, column], axis=0)
        combined = combined + norm_gates[:, column : column + 1] * picked.astype(jnp.float32)
    teacher_out = combined.astype(jnp.bfloat16)
    return finish(teacher_out, projector, student, target_mask)


MESH = pl.DeviceIdType.MESH


def over_rows(count, step, work):
    def one(i, carry):
        work(pl.ds(pl.multiple_of(i * step, step), step))
        return carry

    lax.fori_loop(0, count // step, one, 0)


def fused_kernel(
    expert_axis,
    grad_scale,
    tokens_ref,
    ids_ref,
    scores_ref,
    gate_ref,
    up_ref,
    down_ref,
    projector_ref,
    student_ref,
    mask_ref,
    projected_ref,
    grad_ref,
    tok,
    gate_up,
    down,
    acc,
    pair_send,
    pair_recv,
    line_send,
    line_recv,
    teach,
    error,
    grad_acc,
    gpair_send,
    gpair_recv,
    gline_send,
    gline_recv,
    tok_send_sem,
    tok_recv_sem,
    w_send_sem,
    w_recv_sem,
    pair_sem,
    line_sem,
    teach_send_sem,
    teach_recv_sem,
    gpair_sem,
    gline_sem,
):
    rows, width = tokens_ref.shape
    top_count = ids_ref.shape[1]
    half = gate_ref.shape[2]
    features = projector_ref.shape[1]
    line = expert_axis // 2
    e = lax.axis_index("expert")
    d = lax.axis_index("dp")
    z, y = e // 2, e % 2
    x, c = d // 2, d % 2
    peer = e + 1 - 2 * y
    mate = d + 1 - 2 * c
    cross = d + 2 - 4 * x
    diagonal = cross + 1 - 2 * c
    has_low, has_high = z > 0, z < line - 1

    def remote(src, dst, send, recv, to_e, to_d):
        return pltpu.make_async_remote_copy(
            src_ref=src, dst_ref=dst, send_sem=send, recv_sem=recv,
            device_id={"expert": to_e, "dp": to_d}, device_id_type=MESH,
        )

    barrier = pltpu.get_barrier_semaphore()

    def greet(to_e, to_d):
        pl.semaphore_signal(
            barrier, inc=1, device_id={"expert": to_e, "dp": to_d}, device_id_type=MESH
        )

    greet(peer, d)
    greet(e, mate)
    greet(e, cross)

    @pl.when(has_low)
    def _():
        greet(e - 2, d)

    @pl.when(has_high)
    def _():
        greet(e + 2, d)

    ends = jnp.where(z == 0, 1, 0) + jnp.where(z == line - 1, 1, 0)
    pl.semaphore_wait(barrier, 5 - ends)

    def tok_copy(row, way):
        slot = 2 * row + y
        to_e = (e + 2, e - 2, peer)[way]
        return remote(
            tok.at[slot], tok.at[slot], tok_send_sem.at[row, way], tok_recv_sem.at[slot], to_e, d
        )

    def tok_arrived(slot):
        remote(
            tok.at[slot], tok.at[slot], tok_send_sem.at[0, 0], tok_recv_sem.at[slot], peer, d
        ).wait_recv()

    scores = scores_ref[...]
    norm = scores / jnp.sum(scores, axis=1, keepdims=True)
    ids = ids_ref[...]
    lane = lax.broadcasted_iota(jnp.int32, (rows, 128), 1)
    named = lane % 64
    dense = jnp.zeros((rows, 128), jnp.float32)
    for j in range(top_count):
        dense = dense + jnp.where(ids[:, j : j + 1] == named, norm[:, j : j + 1], 0.0)
    coarse = dense.astype(jnp.bfloat16).astype(jnp.float32)
    tok[e, :, width : width + 128] = jnp.where(lane < 64, coarse, dense - coarse).astype(jnp.bfloat16)
    tok[e, :, 0:width] = tokens_ref[...]

    @pl.when(has_high)
    def _():
        tok_copy(z, 0).start()

    @pl.when(has_low)
    def _():
        tok_copy(z, 1).start()

    tok_copy(z, 2).start()

    def w_copy(piece, slab, way):
        if piece < 2:
            part = pl.ds(piece * (width // 2), width // 2)
            ref = gate_up.at[slab, part]
        else:
            ref = down.at[slab]
        return remote(
            ref, ref, w_send_sem.at[piece, way], w_recv_sem.at[piece, slab], e,
            (cross, mate, mate)[way],
        )

    for piece in range(2):
        def join(part, piece=piece):
            at = pl.ds(pl.multiple_of(piece * (width // 2) + part.start, 128), 128)
            gate_up[d, at, 0:half] = gate_ref[0, at, :]
            gate_up[d, at, half : 2 * half] = up_ref[0, at, :]

        over_rows(width // 2, 128, join)
        w_copy(piece, d, 0).start()
        w_copy(piece, d, 1).start()
    down[d] = down_ref[0]
    w_copy(2, d, 0).start()
    w_copy(2, d, 1).start()

    def expert_on(row, chip, first):
        base = 2 * chip
        expert = 2 * e + chip
        block = tok[pl.ds(2 * row, 2), :, 0:width].reshape(2 * rows, width)
        hidden = []
        for part in range(2):
            both = jnp.dot(block, gate_up[base + part], preferred_element_type=jnp.float32)
            pre, up = both[:, 0:half], both[:, half : 2 * half]
            hidden.append((pre / (1.0 + jnp.exp(-pre)) * up).astype(jnp.bfloat16))
        gates = tok[pl.ds(2 * row, 2), :, width : width + 128].astype(jnp.float32)
        gates = gates.reshape(2 * rows, 128)
        which = lax.broadcasted_iota(jnp.int32, (2 * rows, 128), 1) % 64
        gate = jnp.sum(jnp.where(which == expert, gates, 0.0), axis=1, keepdims=True)
        span = 512

        def columns(i, carry):
            at = pl.ds(pl.multiple_of(i * span, span), span)
            out = jnp.dot(hidden[0], down[base, :, at], preferred_element_type=jnp.float32)
            out += jnp.dot(hidden[1], down[base + 1, :, at], preferred_element_type=jnp.float32)
            out = gate * out.astype(jnp.bfloat16).astype(jnp.float32)
            out = out.reshape(2, rows, span)
            if first:
                acc[pl.ds(2 * row, 2), :, at] = out
            else:
                acc[pl.ds(2 * row, 2), :, at] += out
            return carry

        lax.fori_loop(0, width // span, columns, 0)

    def near_first(j, carry):
        reach, side = (j + 1) // 2, j % 2
        row = z + reach * (1 - 2 * side)

        @pl.when(jnp.logical_and(row >= 0, row < line))
        def _():
            @pl.when(row != z)
            def _():
                tok_arrived(2 * row + y)

                @pl.when(jnp.logical_and(row < z, has_high))
                def _():
                    tok_copy(row, 0).start()

                @pl.when(jnp.logical_and(row > z, has_low))
                def _():
                    tok_copy(row, 1).start()

                tok_copy(row, 2).start()

            @pl.when(row == z)
            def _():
                for piece in range(3):
                    w_copy(piece, mate, 1).wait_recv()

            tok_arrived(2 * row + 1 - y)
            expert_on(row, x, True)

        return carry

    lax.fori_loop(0, 2 * line - 1, near_first, 0)
    for piece in range(3):
        w_copy(piece, cross, 1).wait_recv()
        w_copy(piece, cross, 2).start()
    for piece in range(3):
        w_copy(piece, diagonal, 1).wait_recv()

    def place(p):
        k = line - 1 - p
        return 2 * ((z // 2 + k // 2) % (line // 2)) + (z + k) % 2

    def sum_over_experts(total, psend, precv, lsend, lrecv, psem, lsem, make, step, write):
        count = total.shape[1]

        def pair_copy(row):
            return remote(psend.at[row], precv.at[row], psem.at[0, row], psem.at[1, row], peer, d)

        def line_copy(way, row):
            return remote(
                lsend.at[way, row], lrecv.at[way, row], lsem.at[0, way, row],
                lsem.at[1, way, row], e + 2 - 4 * way, d,
            )

        def produce(p, carry):
            row = place(p)
            make(row)

            def narrow(part):
                psend[row, part] = total[2 * row + 1 - y, part].astype(jnp.bfloat16)

            over_rows(count, step, narrow)
            pair_copy(row).start()
            return carry

        lax.fori_loop(0, line, produce, 0)

        def pass_on(p, carry):
            row = place(p)
            own = 2 * row + y
            pair_copy(row).wait_recv()

            def add_pair(part):
                total[own, part] += precv[row, part].astype(jnp.float32)

            over_rows(count, step, add_pair)

            for way, before, beyond in ((0, has_low, row >= z), (1, has_high, row <= z)):
                @pl.when(jnp.logical_and(before, beyond))
                def _():
                    line_copy(way, row).wait_recv()

                    def add_line(part):
                        total[own, part] += lrecv[way, row, part].astype(jnp.float32)

                    over_rows(count, step, add_line)

            for way, further in ((0, row > z), (1, row < z)):
                @pl.when(further)
                def _():
                    def narrow(part):
                        lsend[way, row, part] = total[own, part].astype(jnp.bfloat16)

                    over_rows(count, step, narrow)
                    line_copy(way, row).start()

            return carry

        lax.fori_loop(0, line, pass_on, 0)

        def finish_row(part):
            write(part, total[e, part])

        over_rows(count, step, finish_row)

        def settle(row, carry):
            pair_copy(row).wait_send()
            for way, further in ((0, row > z), (1, row < z)):
                @pl.when(further)
                def _():
                    line_copy(way, row).wait_send()
            return carry

        lax.fori_loop(0, line, settle, 0)

    def write_teacher(part, value):
        teach[d, part] = value.astype(jnp.bfloat16)

    sum_over_experts(
        acc, pair_send, pair_recv, line_send, line_recv, pair_sem, line_sem,
        lambda row: expert_on(row, 1 - x, False), 32, write_teacher,
    )

    def teach_copy(block, way):
        return remote(
            teach.at[block], teach.at[block], teach_send_sem.at[way], teach_recv_sem.at[block], e,
            (cross, mate, mate)[way],
        )

    def project(block):
        at = pl.ds(pl.multiple_of(block * rows, rows), rows)
        value = jnp.dot(teach[block], projector_ref[...], preferred_element_type=jnp.float32)
        projected_ref[at, :] = value.astype(jnp.bfloat16)
        gap = value - student_ref[at, :].astype(jnp.float32)
        error[at, :] = (mask_ref[at, :].astype(jnp.float32) * gap).astype(jnp.bfloat16)

    teach_copy(d, 0).start()
    teach_copy(d, 1).start()
    project(d)
    teach_copy(mate, 1).wait_recv()
    project(mate)
    teach_copy(cross, 1).wait_recv()
    teach_copy(cross, 2).start()
    project(cross)
    teach_copy(diagonal, 1).wait_recv()
    project(diagonal)

    share = grad_acc.shape[1]
    blocks = teach.shape[0]

    def grad_of(row):
        def one(side, carry):
            target = 2 * row + side
            at = pl.ds(pl.multiple_of(target * share, share), share)
            grad_acc[target] = lax.dot_general(
                teach[:, :, at].reshape(blocks * rows, share), error[...],
                (((0,), (0,)), ((), ())), preferred_element_type=jnp.float32,
            )
            return carry

        lax.fori_loop(0, 2, one, 0)

    def write_grad(part, value):
        grad_ref[part, :] = value * grad_scale

    sum_over_experts(
        grad_acc, gpair_send, gpair_recv, gline_send, gline_recv, gpair_sem, gline_sem,
        grad_of, 64, write_grad,
    )

    def settle(row, carry):
        @pl.when(jnp.logical_and(row <= z, has_high))
        def _():
            tok_copy(row, 0).wait_send()

        @pl.when(jnp.logical_and(row >= z, has_low))
        def _():
            tok_copy(row, 1).wait_send()

        tok_copy(row, 2).wait_send()
        return carry

    lax.fori_loop(0, line, settle, 0)
    for piece in range(3):
        w_copy(piece, d, 0).wait_send()
        w_copy(piece, d, 1).wait_send()
        w_copy(piece, cross, 2).wait_send()
    teach_copy(d, 0).wait_send()
    teach_copy(d, 1).wait_send()
    teach_copy(cross, 2).wait_send()


def fused_body(tokens, expert_ids, gate_scores, w_gate, w_up, w_down, projector, student, target_mask):
    rows, width = tokens.shape
    expert_axis, data_axis = lax.axis_size("expert"), lax.axis_size("dp")
    half, features = w_gate.shape[2], projector.shape[1]
    line, share = expert_axis // 2, width // expert_axis
    grad_scale = 1.0 / math.sqrt(rows * expert_axis * data_axis)
    bf16, f32 = jnp.bfloat16, jnp.float32
    dma = pltpu.SemaphoreType.DMA
    vmem = pl.BlockSpec(memory_space=pltpu.VMEM)
    return pl.pallas_call(
        functools.partial(fused_kernel, expert_axis, grad_scale),
        out_shape=(
            jax.ShapeDtypeStruct(student.shape, bf16),
            jax.ShapeDtypeStruct((share, features), f32),
        ),
        in_specs=[vmem] * 9,
        out_specs=(vmem, vmem),
        scratch_shapes=[
            pltpu.VMEM((expert_axis, rows, width + 128), bf16),
            pltpu.VMEM((data_axis, width, 2 * half), bf16),
            pltpu.VMEM((data_axis, half, width), bf16),
            pltpu.VMEM((expert_axis, rows, width), f32),
            pltpu.VMEM((line, rows, width), bf16),
            pltpu.VMEM((line, rows, width), bf16),
            pltpu.VMEM((2, line, rows, width), bf16),
            pltpu.VMEM((2, line, rows, width), bf16),
            pltpu.VMEM((data_axis, rows, width), bf16),
            pltpu.VMEM((data_axis * rows, features), bf16),
            pltpu.VMEM((expert_axis, share, features), f32),
            pltpu.VMEM((line, share, features), bf16),
            pltpu.VMEM((line, share, features), bf16),
            pltpu.VMEM((2, line, share, features), bf16),
            pltpu.VMEM((2, line, share, features), bf16),
            dma((line, 3)),
            dma((expert_axis,)),
            dma((3, 3)),
            dma((3, data_axis)),
            dma((2, line)),
            dma((2, 2, line)),
            dma((3,)),
            dma((data_axis,)),
            dma((2, line)),
            dma((2, 2, line)),
        ],
        compiler_params=pltpu.CompilerParams(
            collective_id=0, has_side_effects=True, vmem_limit_bytes=60 * 1024 * 1024
        ),
    )(
        tokens, expert_ids, gate_scores, w_gate, w_up, w_down, projector, student,
        target_mask.reshape(-1, 1),
    )


def finish(teacher_out, projector, student, target_mask):
    grad_scale = 1.0 / math.sqrt(teacher_out.shape[0] * lax.axis_size("expert") * lax.axis_size("dp"))
    mask_rows = target_mask.astype(jnp.float32)
    portion = lax.all_gather(teacher_out, "dp", axis=0, tiled=True)
    proj_part = jnp.dot(portion, projector, preferred_element_type=jnp.float32)
    target_part = student.astype(jnp.float32)
    error_part = (mask_rows[:, None] * (proj_part - target_part)).astype(jnp.bfloat16)
    grad_term = lax.dot_general(
        portion, error_part, (((0,), (0,)), ((), ())), preferred_element_type=jnp.float32
    )
    grad_part = (
        lax.psum_scatter(
            grad_term.astype(jnp.bfloat16), "expert", scatter_dimension=0, tiled=True
        ).astype(jnp.float32)
        * grad_scale
    )
    return (proj_part.astype(jnp.bfloat16), grad_part)


def solution(mesh):
    fits = mesh.shape["expert"] == 8 and mesh.shape["dp"] == 4
    body = fused_body if fits else routed_body
    return jax.shard_map(
        body,
        mesh=mesh,
        in_specs=(
            P(("groups", "expert", "dp"), None),
            P(("groups", "expert", "dp"), None),
            P(("groups", "expert", "dp"), None),
            P(("expert", "dp"), None, None),
            P(("expert", "dp"), None, None),
            P(("expert", "dp"), None, None),
            P(None, "dp"),
            P(("groups", "expert"), "dp"),
            P(("groups", "expert")),
        ),
        out_specs=(P(("groups", "expert"), "dp"), P(("groups", "expert"), "dp")),
        check_vma=False,
    )
```

```python
import functools
import math

import jax
import jax.numpy as jnp
from jax import lax
from jax.experimental import pallas as pl
from jax.experimental.pallas import tpu as pltpu
from jax.sharding import PartitionSpec as P


def from_partner(block, axis, apart):
    count = lax.axis_size(axis)
    route = []
    for low in range(count):
        high = low | 1 << apart
        if high != low and high < count:
            route += [(low, high), (high, low)]
    return lax.ppermute(block, axis, route)


def half_hidden(slot_rows, gate_half, up_half):
    gate_pre = jnp.dot(slot_rows, gate_half, preferred_element_type=jnp.float32)
    up_pre = jnp.dot(slot_rows, up_half, preferred_element_type=jnp.float32)
    return (jax.nn.silu(gate_pre) * up_pre).astype(jnp.bfloat16)


def routed_body(tokens, expert_ids, gate_scores, w_gate, w_up, w_down, projector, student, target_mask):
    tok_count = tokens.shape[0]
    model_width = tokens.shape[1]
    top_count = expert_ids.shape[1]
    expert_axis = lax.axis_size("expert")
    data_axis = lax.axis_size("dp")
    expert_total = expert_axis * data_axis // 2
    capacity = min(
        tok_count, 2 * ((3 * tok_count * top_count + 4 * expert_total - 1) // (4 * expert_total))
    )
    half_cap = capacity // 2
    slot_total = expert_total * capacity
    expert_iota = jnp.arange(expert_total, dtype=jnp.int32)
    naming = (expert_ids[:, :, None] == expert_iota[None, None, :]).astype(jnp.int32)
    expert_hits = jnp.sum(naming, axis=1)
    earlier = jnp.cumsum(expert_hits, axis=0) - expert_hits
    slot_index = jnp.sum(naming * earlier[:, None, :], axis=2)
    position = expert_ids * capacity + slot_index
    token_iota = jnp.broadcast_to(
        jnp.arange(tok_count, dtype=jnp.int32)[:, None], (tok_count, top_count)
    )
    slot_table = (
        jnp.full((slot_total,), tok_count, jnp.int32)
        .at[position.reshape(-1)]
        .set(token_iota.reshape(-1))
    )
    padded_tokens = jnp.concatenate([tokens, jnp.zeros((1, model_width), tokens.dtype)], axis=0)
    send_rows = jnp.take(padded_tokens, slot_table, axis=0)
    send_rows = send_rows.reshape(expert_axis, data_axis, half_cap, model_width)
    arrived = lax.all_to_all(
        lax.all_to_all(send_rows, "expert", split_axis=0, concat_axis=0, tiled=True),
        "dp",
        split_axis=1,
        concat_axis=1,
        tiled=True,
    )
    slot_rows = arrived.reshape(slot_total, model_width)
    gate_mine = w_gate[0]
    up_mine = w_up[0]
    down_mine = w_down[0]
    gate_other, up_other, down_other = from_partner((gate_mine, up_mine, down_mine), "dp", 0)
    hidden_mine = half_hidden(slot_rows, gate_mine, up_mine)
    hidden_other = half_hidden(slot_rows, gate_other, up_other)
    expert_out = (
        jnp.dot(hidden_mine, down_mine, preferred_element_type=jnp.float32)
        + jnp.dot(hidden_other, down_other, preferred_element_type=jnp.float32)
    ).astype(jnp.bfloat16)
    came_back = lax.all_to_all(
        lax.all_to_all(
            expert_out.reshape(expert_axis, data_axis, half_cap, model_width),
            "expert",
            split_axis=0,
            concat_axis=0,
            tiled=True,
        ),
        "dp",
        split_axis=1,
        concat_axis=1,
        tiled=True,
    )
    returned = came_back.reshape(slot_total, model_width)
    norm_gates = gate_scores / jnp.sum(gate_scores, axis=1, keepdims=True)
    combined = jnp.zeros((tok_count, model_width), jnp.float32)
    for column in range(top_count):
        picked = jnp.take(returned, position[:, column], axis=0)
        combined = combined + norm_gates[:, column : column + 1] * picked.astype(jnp.float32)
    teacher_out = combined.astype(jnp.bfloat16)
    return finish(teacher_out, projector, student, target_mask)


MESH = pl.DeviceIdType.MESH


def over_rows(count, step, work):
    def one(i, carry):
        work(pl.ds(pl.multiple_of(i * step, step), step))
        return carry

    lax.fori_loop(0, count // step, one, 0)


def fused_kernel(
    expert_axis,
    grad_scale,
    tokens_ref,
    ids_ref,
    scores_ref,
    gate_ref,
    up_ref,
    down_ref,
    projector_ref,
    student_ref,
    mask_ref,
    projected_ref,
    grad_ref,
    tok,
    gate_up,
    down,
    acc,
    pair_send,
    pair_recv,
    line_send,
    line_recv,
    teach,
    error,
    grad_acc,
    gpair_send,
    gpair_recv,
    gline_send,
    gline_recv,
    tok_send_sem,
    tok_recv_sem,
    w_send_sem,
    w_recv_sem,
    pair_sem,
    line_sem,
    teach_send_sem,
    teach_recv_sem,
    gpair_sem,
    gline_sem,
):
    rows, width = tokens_ref.shape
    top_count = ids_ref.shape[0]
    half = gate_ref.shape[1]
    features = projector_ref.shape[1]
    line = expert_axis // 2
    e = lax.axis_index("expert")
    d = lax.axis_index("dp")
    z, y = e // 2, e % 2
    x, c = d // 2, d % 2
    peer = e + 1 - 2 * y
    mate = d + 1 - 2 * c
    cross = d + 2 - 4 * x
    diagonal = cross + 1 - 2 * c
    has_low, has_high = z > 0, z < line - 1

    def remote(src, dst, send, recv, to_e, to_d):
        return pltpu.make_async_remote_copy(
            src_ref=src, dst_ref=dst, send_sem=send, recv_sem=recv,
            device_id={"expert": to_e, "dp": to_d}, device_id_type=MESH,
        )

    barrier = pltpu.get_barrier_semaphore()

    def greet(to_e, to_d):
        pl.semaphore_signal(
            barrier, inc=1, device_id={"expert": to_e, "dp": to_d}, device_id_type=MESH
        )

    greet(peer, d)
    greet(e, mate)
    greet(e, cross)

    @pl.when(has_low)
    def _():
        greet(e - 2, d)

    @pl.when(has_high)
    def _():
        greet(e + 2, d)

    ends = jnp.where(z == 0, 1, 0) + jnp.where(z == line - 1, 1, 0)
    pl.semaphore_wait(barrier, 5 - ends)

    def tok_copy(row, way):
        slot = 2 * row + y
        to_e = (e + 2, e - 2, peer)[way]
        return remote(
            tok.at[slot], tok.at[slot], tok_send_sem.at[row, way], tok_recv_sem.at[slot], to_e, d
        )

    def tok_arrived(slot):
        remote(
            tok.at[slot], tok.at[slot], tok_send_sem.at[0, 0], tok_recv_sem.at[slot], peer, d
        ).wait_recv()

    scores = scores_ref[...]
    norm = scores / jnp.sum(scores, axis=0, keepdims=True)
    ids = ids_ref[...]
    named = lax.broadcasted_iota(jnp.int32, (128, rows), 0) % 64
    dense = jnp.zeros((128, rows), jnp.float32)
    for j in range(top_count):
        dense = dense + jnp.where(ids[j : j + 1, :] == named, norm[j : j + 1, :], 0.0)
    dense = dense.T
    lane = lax.broadcasted_iota(jnp.int32, (rows, 128), 1)
    coarse = dense.astype(jnp.bfloat16).astype(jnp.float32)
    tok[e, :, width : width + 128] = jnp.where(lane < 64, coarse, dense - coarse).astype(jnp.bfloat16)
    tok[e, :, 0:width] = tokens_ref[...]

    @pl.when(has_high)
    def _():
        tok_copy(z, 0).start()

    @pl.when(has_low)
    def _():
        tok_copy(z, 1).start()

    tok_copy(z, 2).start()

    def w_copy(piece, slab, way):
        if piece < 2:
            ref = gate_up.at[slab, pl.ds(piece * half, half)]
        else:
            ref = down.at[slab]
        return remote(
            ref, ref, w_send_sem.at[piece, way], w_recv_sem.at[piece, slab], e,
            (cross, mate, mate)[way],
        )

    gate_up[d, 0:half] = gate_ref[0]
    w_copy(0, d, 0).start()
    w_copy(0, d, 1).start()
    gate_up[d, half : 2 * half] = up_ref[0]
    w_copy(1, d, 0).start()
    w_copy(1, d, 1).start()
    down[d] = down_ref[0]
    w_copy(2, d, 0).start()
    w_copy(2, d, 1).start()

    def expert_on(row, chip, first):
        base = 2 * chip
        expert = 2 * e + chip
        block = tok[pl.ds(2 * row, 2), :, 0:width].reshape(2 * rows, width)
        hidden = []
        for part in range(2):
            both = lax.dot_general(
                block, gate_up[base + part], (((1,), (1,)), ((), ())),
                preferred_element_type=jnp.float32,
            )
            pre, up = both[:, 0:half], both[:, half : 2 * half]
            hidden.append((pre / (1.0 + jnp.exp(-pre)) * up).astype(jnp.bfloat16))
        gates = tok[pl.ds(2 * row, 2), :, width : width + 128].astype(jnp.float32)
        gates = gates.reshape(2 * rows, 128)
        which = lax.broadcasted_iota(jnp.int32, (2 * rows, 128), 1) % 64
        gate = jnp.sum(jnp.where(which == expert, gates, 0.0), axis=1, keepdims=True)
        span = 512

        def columns(i, carry):
            at = pl.ds(pl.multiple_of(i * span, span), span)
            out = jnp.dot(hidden[0], down[base, :, at], preferred_element_type=jnp.float32)
            out += jnp.dot(hidden[1], down[base + 1, :, at], preferred_element_type=jnp.float32)
            out = gate * out.astype(jnp.bfloat16).astype(jnp.float32)
            out = out.reshape(2, rows, span)
            if first:
                acc[pl.ds(2 * row, 2), :, at] = out
            else:
                acc[pl.ds(2 * row, 2), :, at] += out
            return carry

        lax.fori_loop(0, width // span, columns, 0)

    def near_first(reach, carry):
        for side in (-1, 1):
            row = z + side * (reach + 1)

            @pl.when(jnp.logical_and(row >= 0, row < line))
            def _():
                tok_arrived(2 * row + y)

                @pl.when(has_high if side < 0 else has_low)
                def _():
                    tok_copy(row, (1 + side) // 2).start()

                tok_copy(row, 2).start()

        @pl.when(reach == 0)
        def _():
            for piece in range(3):
                w_copy(piece, mate, 1).wait_recv()

        def one_side(side, inner):
            row = z + reach * (2 * side - 1)

            @pl.when(
                jnp.logical_and(jnp.logical_and(row >= 0, row < line), reach + side > 0)
            )
            def _():
                tok_arrived(2 * row + 1 - y)
                expert_on(row, x, True)

            return inner

        lax.fori_loop(0, 2, one_side, 0)
        return carry

    lax.fori_loop(0, line, near_first, 0)
    for piece in range(3):
        w_copy(piece, cross, 1).wait_recv()
        w_copy(piece, cross, 2).start()
    for piece in range(3):
        w_copy(piece, diagonal, 1).wait_recv()

    def place(p):
        k = line - 1 - p
        return 2 * ((z // 2 + k // 2) % (line // 2)) + (z + k) % 2

    def sum_over_experts(total, psend, precv, lsend, lrecv, psem, lsem, make, step, write):
        count = total.shape[1]

        def pair_copy(row):
            return remote(psend.at[row], precv.at[row], psem.at[0, row], psem.at[1, row], peer, d)

        def line_copy(way, row):
            return remote(
                lsend.at[way, row], lrecv.at[way, row], lsem.at[0, way, row],
                lsem.at[1, way, row], e + 2 - 4 * way, d,
            )

        def produce(p, carry):
            row = place(p)
            make(row)

            def narrow(part):
                psend[row, part] = total[2 * row + 1 - y, part].astype(jnp.bfloat16)

            over_rows(count, step, narrow)
            pair_copy(row).start()
            return carry

        lax.fori_loop(0, line, produce, 0)

        def pass_on(p, carry):
            row = place(p)
            own = 2 * row + y
            pair_copy(row).wait_recv()

            def add_pair(part):
                total[own, part] += precv[row, part].astype(jnp.float32)

            over_rows(count, step, add_pair)

            for way, before, beyond in ((0, has_low, row >= z), (1, has_high, row <= z)):
                @pl.when(jnp.logical_and(before, beyond))
                def _():
                    line_copy(way, row).wait_recv()

                    def add_line(part):
                        total[own, part] += lrecv[way, row, part].astype(jnp.float32)

                    over_rows(count, step, add_line)

            for way, further in ((0, row > z), (1, row < z)):
                @pl.when(further)
                def _():
                    def narrow(part):
                        lsend[way, row, part] = total[own, part].astype(jnp.bfloat16)

                    over_rows(count, step, narrow)
                    line_copy(way, row).start()

            return carry

        lax.fori_loop(0, line, pass_on, 0)

        def finish_row(part):
            write(part, total[e, part])

        over_rows(count, step, finish_row)

        def settle(row, carry):
            pair_copy(row).wait_send()
            for way, further in ((0, row > z), (1, row < z)):
                @pl.when(further)
                def _():
                    line_copy(way, row).wait_send()
            return carry

        lax.fori_loop(0, line, settle, 0)

    def write_teacher(part, value):
        teach[d, part] = value.astype(jnp.bfloat16)

    sum_over_experts(
        acc, pair_send, pair_recv, line_send, line_recv, pair_sem, line_sem,
        lambda row: expert_on(row, 1 - x, False), 32, write_teacher,
    )

    def teach_copy(block, way):
        return remote(
            teach.at[block], teach.at[block], teach_send_sem.at[way], teach_recv_sem.at[block], e,
            (cross, mate, mate)[way],
        )

    def project(block):
        at = pl.ds(pl.multiple_of(block * rows, rows), rows)
        value = jnp.dot(teach[block], projector_ref[...], preferred_element_type=jnp.float32)
        projected_ref[at, :] = value.astype(jnp.bfloat16)
        gap = value - student_ref[at, :].astype(jnp.float32)
        mask = jnp.broadcast_to(mask_ref[:, at].astype(jnp.float32), (128, rows)).T[:, 0:1]
        error[at, :] = (mask * gap).astype(jnp.bfloat16)

    teach_copy(d, 0).start()
    teach_copy(d, 1).start()
    project(d)
    teach_copy(mate, 1).wait_recv()
    project(mate)
    teach_copy(cross, 1).wait_recv()
    teach_copy(cross, 2).start()
    project(cross)
    teach_copy(diagonal, 1).wait_recv()
    project(diagonal)

    share = grad_acc.shape[1]
    blocks = teach.shape[0]

    def grad_of(row):
        def one(side, carry):
            target = 2 * row + side
            at = pl.ds(pl.multiple_of(target * share, share), share)
            grad_acc[target] = lax.dot_general(
                teach[:, :, at].reshape(blocks * rows, share), error[...],
                (((0,), (0,)), ((), ())), preferred_element_type=jnp.float32,
            )
            return carry

        lax.fori_loop(0, 2, one, 0)

    def write_grad(part, value):
        grad_ref[part, :] = value * grad_scale

    sum_over_experts(
        grad_acc, gpair_send, gpair_recv, gline_send, gline_recv, gpair_sem, gline_sem,
        grad_of, 64, write_grad,
    )

    def settle(row, carry):
        @pl.when(jnp.logical_and(row <= z, has_high))
        def _():
            tok_copy(row, 0).wait_send()

        @pl.when(jnp.logical_and(row >= z, has_low))
        def _():
            tok_copy(row, 1).wait_send()

        tok_copy(row, 2).wait_send()
        return carry

    lax.fori_loop(0, line, settle, 0)
    for piece in range(3):
        w_copy(piece, d, 0).wait_send()
        w_copy(piece, d, 1).wait_send()
        w_copy(piece, cross, 2).wait_send()
    teach_copy(d, 0).wait_send()
    teach_copy(d, 1).wait_send()
    teach_copy(cross, 2).wait_send()


def fused_body(tokens, expert_ids, gate_scores, w_gate, w_up, w_down, projector, student, target_mask):
    rows, width = tokens.shape
    expert_axis, data_axis = lax.axis_size("expert"), lax.axis_size("dp")
    half, features = w_gate.shape[2], projector.shape[1]
    line, share = expert_axis // 2, width // expert_axis
    grad_scale = 1.0 / math.sqrt(rows * expert_axis * data_axis)
    bf16, f32 = jnp.bfloat16, jnp.float32
    dma = pltpu.SemaphoreType.DMA
    vmem = pl.BlockSpec(memory_space=pltpu.VMEM)
    return pl.pallas_call(
        functools.partial(fused_kernel, expert_axis, grad_scale),
        out_shape=(
            jax.ShapeDtypeStruct(student.shape, bf16),
            jax.ShapeDtypeStruct((share, features), f32),
        ),
        in_specs=[vmem] * 9,
        out_specs=(vmem, vmem),
        scratch_shapes=[
            pltpu.VMEM((expert_axis, rows, width + 128), bf16),
            pltpu.VMEM((data_axis, 2 * half, width), bf16),
            pltpu.VMEM((data_axis, half, width), bf16),
            pltpu.VMEM((expert_axis, rows, width), f32),
            pltpu.VMEM((line, rows, width), bf16),
            pltpu.VMEM((line, rows, width), bf16),
            pltpu.VMEM((2, line, rows, width), bf16),
            pltpu.VMEM((2, line, rows, width), bf16),
            pltpu.VMEM((data_axis, rows, width), bf16),
            pltpu.VMEM((data_axis * rows, features), bf16),
            pltpu.VMEM((expert_axis, share, features), f32),
            pltpu.VMEM((line, share, features), bf16),
            pltpu.VMEM((line, share, features), bf16),
            pltpu.VMEM((2, line, share, features), bf16),
            pltpu.VMEM((2, line, share, features), bf16),
            dma((line, 3)),
            dma((expert_axis,)),
            dma((3, 3)),
            dma((3, data_axis)),
            dma((2, line)),
            dma((2, 2, line)),
            dma((3,)),
            dma((data_axis,)),
            dma((2, line)),
            dma((2, 2, line)),
        ],
        compiler_params=pltpu.CompilerParams(
            collective_id=0, has_side_effects=True, vmem_limit_bytes=60 * 1024 * 1024
        ),
    )(
        tokens, expert_ids.T, gate_scores.T, jnp.swapaxes(w_gate, 1, 2),
        jnp.swapaxes(w_up, 1, 2), w_down, projector, student, target_mask.reshape(1, -1),
    )


def finish(teacher_out, projector, student, target_mask):
    grad_scale = 1.0 / math.sqrt(teacher_out.shape[0] * lax.axis_size("expert") * lax.axis_size("dp"))
    mask_rows = target_mask.astype(jnp.float32)
    portion = lax.all_gather(teacher_out, "dp", axis=0, tiled=True)
    proj_part = jnp.dot(portion, projector, preferred_element_type=jnp.float32)
    target_part = student.astype(jnp.float32)
    error_part = (mask_rows[:, None] * (proj_part - target_part)).astype(jnp.bfloat16)
    grad_term = lax.dot_general(
        portion, error_part, (((0,), (0,)), ((), ())), preferred_element_type=jnp.float32
    )
    grad_part = (
        lax.psum_scatter(
            grad_term.astype(jnp.bfloat16), "expert", scatter_dimension=0, tiled=True
        ).astype(jnp.float32)
        * grad_scale
    )
    return (proj_part.astype(jnp.bfloat16), grad_part)


def solution(mesh):
    fits = mesh.shape["expert"] == 8 and mesh.shape["dp"] == 4
    body = fused_body if fits else routed_body
    return jax.shard_map(
        body,
        mesh=mesh,
        in_specs=(
            P(("groups", "expert", "dp"), None),
            P(("groups", "expert", "dp"), None),
            P(("groups", "expert", "dp"), None),
            P(("expert", "dp"), None, None),
            P(("expert", "dp"), None, None),
            P(("expert", "dp"), None, None),
            P(None, "dp"),
            P(("groups", "expert"), "dp"),
            P(("groups", "expert")),
        ),
        out_specs=(P(("groups", "expert"), "dp"), P(("groups", "expert"), "dp")),
        check_vma=False,
    )
```

```python
import functools
import math

import jax
import jax.numpy as jnp
from jax import lax
from jax.experimental import pallas as pl
from jax.experimental.pallas import tpu as pltpu
from jax.sharding import PartitionSpec as P


def from_partner(block, axis, apart):
    count = lax.axis_size(axis)
    route = []
    for low in range(count):
        high = low | 1 << apart
        if high != low and high < count:
            route += [(low, high), (high, low)]
    return lax.ppermute(block, axis, route)


def half_hidden(slot_rows, gate_half, up_half):
    gate_pre = jnp.dot(slot_rows, gate_half, preferred_element_type=jnp.float32)
    up_pre = jnp.dot(slot_rows, up_half, preferred_element_type=jnp.float32)
    return (jax.nn.silu(gate_pre) * up_pre).astype(jnp.bfloat16)


def routed_body(tokens, expert_ids, gate_scores, w_gate, w_up, w_down, projector, student, target_mask):
    tok_count = tokens.shape[0]
    model_width = tokens.shape[1]
    top_count = expert_ids.shape[1]
    expert_axis = lax.axis_size("expert")
    data_axis = lax.axis_size("dp")
    expert_total = expert_axis * data_axis // 2
    capacity = min(
        tok_count, 2 * ((3 * tok_count * top_count + 4 * expert_total - 1) // (4 * expert_total))
    )
    half_cap = capacity // 2
    slot_total = expert_total * capacity
    expert_iota = jnp.arange(expert_total, dtype=jnp.int32)
    naming = (expert_ids[:, :, None] == expert_iota[None, None, :]).astype(jnp.int32)
    expert_hits = jnp.sum(naming, axis=1)
    earlier = jnp.cumsum(expert_hits, axis=0) - expert_hits
    slot_index = jnp.sum(naming * earlier[:, None, :], axis=2)
    position = expert_ids * capacity + slot_index
    token_iota = jnp.broadcast_to(
        jnp.arange(tok_count, dtype=jnp.int32)[:, None], (tok_count, top_count)
    )
    slot_table = (
        jnp.full((slot_total,), tok_count, jnp.int32)
        .at[position.reshape(-1)]
        .set(token_iota.reshape(-1))
    )
    padded_tokens = jnp.concatenate([tokens, jnp.zeros((1, model_width), tokens.dtype)], axis=0)
    send_rows = jnp.take(padded_tokens, slot_table, axis=0)
    send_rows = send_rows.reshape(expert_axis, data_axis, half_cap, model_width)
    arrived = lax.all_to_all(
        lax.all_to_all(send_rows, "expert", split_axis=0, concat_axis=0, tiled=True),
        "dp",
        split_axis=1,
        concat_axis=1,
        tiled=True,
    )
    slot_rows = arrived.reshape(slot_total, model_width)
    gate_mine = w_gate[0]
    up_mine = w_up[0]
    down_mine = w_down[0]
    gate_other, up_other, down_other = from_partner((gate_mine, up_mine, down_mine), "dp", 0)
    hidden_mine = half_hidden(slot_rows, gate_mine, up_mine)
    hidden_other = half_hidden(slot_rows, gate_other, up_other)
    expert_out = (
        jnp.dot(hidden_mine, down_mine, preferred_element_type=jnp.float32)
        + jnp.dot(hidden_other, down_other, preferred_element_type=jnp.float32)
    ).astype(jnp.bfloat16)
    came_back = lax.all_to_all(
        lax.all_to_all(
            expert_out.reshape(expert_axis, data_axis, half_cap, model_width),
            "expert",
            split_axis=0,
            concat_axis=0,
            tiled=True,
        ),
        "dp",
        split_axis=1,
        concat_axis=1,
        tiled=True,
    )
    returned = came_back.reshape(slot_total, model_width)
    norm_gates = gate_scores / jnp.sum(gate_scores, axis=1, keepdims=True)
    combined = jnp.zeros((tok_count, model_width), jnp.float32)
    for column in range(top_count):
        picked = jnp.take(returned, position[:, column], axis=0)
        combined = combined + norm_gates[:, column : column + 1] * picked.astype(jnp.float32)
    teacher_out = combined.astype(jnp.bfloat16)
    return finish(teacher_out, projector, student, target_mask)


MESH = pl.DeviceIdType.MESH
SUM_PARTS = 4
GRAD_PARTS = 2


def over_rows(count, step, work):
    def one(i, carry):
        work(pl.ds(pl.multiple_of(i * step, step), step))
        return carry

    lax.fori_loop(0, count // step, one, 0)


def fused_kernel(
    expert_axis,
    grad_scale,
    tokens_ref,
    ids_ref,
    scores_ref,
    gate_ref,
    up_ref,
    down_ref,
    projector_ref,
    student_ref,
    mask_ref,
    projected_ref,
    grad_ref,
    tok,
    gate_up,
    down,
    acc,
    pair_send,
    pair_recv,
    line_send,
    line_recv,
    teach,
    error,
    grad_acc,
    gpair_send,
    gpair_recv,
    gline_send,
    gline_recv,
    tok_send_sem,
    tok_recv_sem,
    w_send_sem,
    w_recv_sem,
    pair_sem,
    line_sem,
    teach_send_sem,
    teach_recv_sem,
    gpair_sem,
    gline_sem,
):
    rows, width = tokens_ref.shape
    top_count = ids_ref.shape[0]
    half = gate_ref.shape[1]
    features = projector_ref.shape[1]
    line = expert_axis // 2
    e = lax.axis_index("expert")
    d = lax.axis_index("dp")
    z, y = e // 2, e % 2
    x, c = d // 2, d % 2
    peer = e + 1 - 2 * y
    mate = d + 1 - 2 * c
    cross = d + 2 - 4 * x
    diagonal = cross + 1 - 2 * c
    has_low, has_high = z > 0, z < line - 1

    def remote(src, dst, send, recv, to_e, to_d):
        return pltpu.make_async_remote_copy(
            src_ref=src, dst_ref=dst, send_sem=send, recv_sem=recv,
            device_id={"expert": to_e, "dp": to_d}, device_id_type=MESH,
        )

    barrier = pltpu.get_barrier_semaphore()

    def greet(to_e, to_d):
        pl.semaphore_signal(
            barrier, inc=1, device_id={"expert": to_e, "dp": to_d}, device_id_type=MESH
        )

    greet(peer, d)
    greet(e, mate)
    greet(e, cross)

    @pl.when(has_low)
    def _():
        greet(e - 2, d)

    @pl.when(has_high)
    def _():
        greet(e + 2, d)

    ends = jnp.where(z == 0, 1, 0) + jnp.where(z == line - 1, 1, 0)
    pl.semaphore_wait(barrier, 5 - ends)

    def tok_copy(row, way):
        slot = 2 * row + y
        to_e = (e + 2, e - 2, peer)[way]
        return remote(
            tok.at[slot], tok.at[slot], tok_send_sem.at[row, way], tok_recv_sem.at[slot], to_e, d
        )

    def tok_arrived(slot):
        remote(
            tok.at[slot], tok.at[slot], tok_send_sem.at[0, 0], tok_recv_sem.at[slot], peer, d
        ).wait_recv()

    scores = scores_ref[...]
    norm = scores / jnp.sum(scores, axis=0, keepdims=True)
    ids = ids_ref[...]
    named = lax.broadcasted_iota(jnp.int32, (128, rows), 0) % 64
    dense = jnp.zeros((128, rows), jnp.float32)
    for j in range(top_count):
        dense = dense + jnp.where(ids[j : j + 1, :] == named, norm[j : j + 1, :], 0.0)
    dense = dense.T
    lane = lax.broadcasted_iota(jnp.int32, (rows, 128), 1)
    coarse = dense.astype(jnp.bfloat16).astype(jnp.float32)
    tok[e, :, width : width + 128] = jnp.where(lane < 64, coarse, dense - coarse).astype(jnp.bfloat16)
    tok[e, :, 0:width] = tokens_ref[...]

    @pl.when(has_high)
    def _():
        tok_copy(z, 0).start()

    @pl.when(has_low)
    def _():
        tok_copy(z, 1).start()

    tok_copy(z, 2).start()

    def w_copy(piece, slab, way):
        if piece < 2:
            ref = gate_up.at[slab, pl.ds(piece * half, half)]
        else:
            ref = down.at[slab]
        return remote(
            ref, ref, w_send_sem.at[piece, way], w_recv_sem.at[piece, slab], e,
            (cross, mate, mate)[way],
        )

    gate_up[d, 0:half] = gate_ref[0]
    w_copy(0, d, 0).start()
    w_copy(0, d, 1).start()
    gate_up[d, half : 2 * half] = up_ref[0]
    w_copy(1, d, 0).start()
    w_copy(1, d, 1).start()
    down[d] = down_ref[0]
    w_copy(2, d, 0).start()
    w_copy(2, d, 1).start()

    def expert_on(row, chip, first):
        base = 2 * chip
        expert = 2 * e + chip
        block = tok[pl.ds(2 * row, 2), :, 0:width].reshape(2 * rows, width)
        hidden = []
        for part in range(2):
            both = lax.dot_general(
                block, gate_up[base + part], (((1,), (1,)), ((), ())),
                preferred_element_type=jnp.float32,
            )
            pre, up = both[:, 0:half], both[:, half : 2 * half]
            hidden.append((pre / (1.0 + jnp.exp(-pre)) * up).astype(jnp.bfloat16))
        gates = tok[pl.ds(2 * row, 2), :, width : width + 128].astype(jnp.float32)
        gates = gates.reshape(2 * rows, 128)
        which = lax.broadcasted_iota(jnp.int32, (2 * rows, 128), 1) % 64
        gate = jnp.sum(jnp.where(which == expert, gates, 0.0), axis=1, keepdims=True)
        span = 512

        def columns(i, carry):
            at = pl.ds(pl.multiple_of(i * span, span), span)
            out = jnp.dot(hidden[0], down[base, :, at], preferred_element_type=jnp.float32)
            out += jnp.dot(hidden[1], down[base + 1, :, at], preferred_element_type=jnp.float32)
            out = gate * out.astype(jnp.bfloat16).astype(jnp.float32)
            out = out.reshape(2, rows, span)
            if first:
                acc[pl.ds(2 * row, 2), :, at] = out
            else:
                acc[pl.ds(2 * row, 2), :, at] += out
            return carry

        lax.fori_loop(0, width // span, columns, 0)

    def near_first(reach, carry):
        for side in (-1, 1):
            row = z + side * (reach + 1)

            @pl.when(jnp.logical_and(row >= 0, row < line))
            def _():
                tok_arrived(2 * row + y)

                @pl.when(has_high if side < 0 else has_low)
                def _():
                    tok_copy(row, (1 + side) // 2).start()

                tok_copy(row, 2).start()

        @pl.when(reach == 0)
        def _():
            for piece in range(3):
                w_copy(piece, mate, 1).wait_recv()

        def one_side(side, inner):
            row = z + reach * (2 * side - 1)

            @pl.when(
                jnp.logical_and(jnp.logical_and(row >= 0, row < line), reach + side > 0)
            )
            def _():
                tok_arrived(2 * row + 1 - y)
                expert_on(row, x, True)

            return inner

        lax.fori_loop(0, 2, one_side, 0)
        return carry

    lax.fori_loop(0, line, near_first, 0)
    for piece in range(3):
        w_copy(piece, cross, 1).wait_recv()
        w_copy(piece, cross, 2).start()
    for piece in range(3):
        w_copy(piece, diagonal, 1).wait_recv()

    def place(p):
        k = line - 1 - p
        return 2 * ((z // 2 + k // 2) % (line // 2)) + (z + k) % 2

    def sum_over_experts(total, psend, precv, lsend, lrecv, psem, lsem, make, parts, step, write):
        count = total.shape[1] // parts

        def piece_at(part):
            return pl.ds(pl.multiple_of(part * count, count), count)

        def pair_copy(row, part):
            at = piece_at(part)
            return remote(
                psend.at[row, at], precv.at[row, at], psem.at[0, row, part],
                psem.at[1, row, part], peer, d,
            )

        def line_copy(way, row, part):
            at = piece_at(part)
            return remote(
                lsend.at[way, row, at], lrecv.at[way, row, at], lsem.at[0, way, row, part],
                lsem.at[1, way, row, part], e + 2 - 4 * way, d,
            )

        def over_piece(part, work):
            def one(i, carry):
                work(pl.ds(pl.multiple_of(part * count + i * step, step), step))
                return carry

            lax.fori_loop(0, count // step, one, 0)

        def produce(p, carry):
            row = place(p)
            make(row)

            def narrow(at):
                psend[row, at] = total[2 * row + 1 - y, at].astype(jnp.bfloat16)

            def send(part, inner):
                over_piece(part, narrow)
                pair_copy(row, part).start()
                return inner

            lax.fori_loop(0, parts, send, 0)
            return carry

        lax.fori_loop(0, line, produce, 0)

        def pass_on(q, carry):
            row, part = place(q // parts), q % parts
            own = 2 * row + y
            pair_copy(row, part).wait_recv()

            def add_pair(at):
                total[own, at] += precv[row, at].astype(jnp.float32)

            over_piece(part, add_pair)

            for way, before, beyond in ((0, has_low, row >= z), (1, has_high, row <= z)):
                @pl.when(jnp.logical_and(before, beyond))
                def _():
                    line_copy(way, row, part).wait_recv()

                    def add_line(at):
                        total[own, at] += lrecv[way, row, at].astype(jnp.float32)

                    over_piece(part, add_line)

            for way, further in ((0, row > z), (1, row < z)):
                @pl.when(further)
                def _():
                    def narrow(at):
                        lsend[way, row, at] = total[own, at].astype(jnp.bfloat16)

                    over_piece(part, narrow)
                    line_copy(way, row, part).start()

            return carry

        lax.fori_loop(0, line * parts, pass_on, 0)

        def finish_row(at):
            write(at, total[e, at])

        over_rows(total.shape[1], step, finish_row)

        def settle(q, carry):
            row, part = q // parts, q % parts
            pair_copy(row, part).wait_send()
            for way, further in ((0, row > z), (1, row < z)):
                @pl.when(further)
                def _():
                    line_copy(way, row, part).wait_send()
            return carry

        lax.fori_loop(0, line * parts, settle, 0)

    def write_teacher(part, value):
        teach[d, part] = value.astype(jnp.bfloat16)

    sum_over_experts(
        acc, pair_send, pair_recv, line_send, line_recv, pair_sem, line_sem,
        lambda row: expert_on(row, 1 - x, False), SUM_PARTS, 16, write_teacher,
    )

    def teach_copy(block, way):
        return remote(
            teach.at[block], teach.at[block], teach_send_sem.at[way], teach_recv_sem.at[block], e,
            (cross, mate, mate)[way],
        )

    def project(block):
        at = pl.ds(pl.multiple_of(block * rows, rows), rows)
        value = jnp.dot(teach[block], projector_ref[...], preferred_element_type=jnp.float32)
        projected_ref[at, :] = value.astype(jnp.bfloat16)
        gap = value - student_ref[at, :].astype(jnp.float32)
        mask = jnp.broadcast_to(mask_ref[:, at].astype(jnp.float32), (128, rows)).T[:, 0:1]
        error[at, :] = (mask * gap).astype(jnp.bfloat16)

    teach_copy(d, 0).start()
    teach_copy(d, 1).start()
    project(d)
    teach_copy(mate, 1).wait_recv()
    project(mate)
    teach_copy(cross, 1).wait_recv()
    teach_copy(cross, 2).start()
    project(cross)
    teach_copy(diagonal, 1).wait_recv()
    project(diagonal)

    share = grad_acc.shape[1]
    blocks = teach.shape[0]

    def grad_of(row):
        def one(side, carry):
            target = 2 * row + side
            at = pl.ds(pl.multiple_of(target * share, share), share)
            grad_acc[target] = lax.dot_general(
                teach[:, :, at].reshape(blocks * rows, share), error[...],
                (((0,), (0,)), ((), ())), preferred_element_type=jnp.float32,
            )
            return carry

        lax.fori_loop(0, 2, one, 0)

    def write_grad(part, value):
        grad_ref[part, :] = value * grad_scale

    sum_over_experts(
        grad_acc, gpair_send, gpair_recv, gline_send, gline_recv, gpair_sem, gline_sem,
        grad_of, GRAD_PARTS, 64, write_grad,
    )

    def settle(row, carry):
        @pl.when(jnp.logical_and(row <= z, has_high))
        def _():
            tok_copy(row, 0).wait_send()

        @pl.when(jnp.logical_and(row >= z, has_low))
        def _():
            tok_copy(row, 1).wait_send()

        tok_copy(row, 2).wait_send()
        return carry

    lax.fori_loop(0, line, settle, 0)
    for piece in range(3):
        w_copy(piece, d, 0).wait_send()
        w_copy(piece, d, 1).wait_send()
        w_copy(piece, cross, 2).wait_send()
    teach_copy(d, 0).wait_send()
    teach_copy(d, 1).wait_send()
    teach_copy(cross, 2).wait_send()


def fused_body(tokens, expert_ids, gate_scores, w_gate, w_up, w_down, projector, student, target_mask):
    rows, width = tokens.shape
    expert_axis, data_axis = lax.axis_size("expert"), lax.axis_size("dp")
    half, features = w_gate.shape[2], projector.shape[1]
    line, share = expert_axis // 2, width // expert_axis
    grad_scale = 1.0 / math.sqrt(rows * expert_axis * data_axis)
    bf16, f32 = jnp.bfloat16, jnp.float32
    dma = pltpu.SemaphoreType.DMA
    vmem = pl.BlockSpec(memory_space=pltpu.VMEM)
    return pl.pallas_call(
        functools.partial(fused_kernel, expert_axis, grad_scale),
        out_shape=(
            jax.ShapeDtypeStruct(student.shape, bf16),
            jax.ShapeDtypeStruct((share, features), f32),
        ),
        in_specs=[vmem] * 9,
        out_specs=(vmem, vmem),
        scratch_shapes=[
            pltpu.VMEM((expert_axis, rows, width + 128), bf16),
            pltpu.VMEM((data_axis, 2 * half, width), bf16),
            pltpu.VMEM((data_axis, half, width), bf16),
            pltpu.VMEM((expert_axis, rows, width), f32),
            pltpu.VMEM((line, rows, width), bf16),
            pltpu.VMEM((line, rows, width), bf16),
            pltpu.VMEM((2, line, rows, width), bf16),
            pltpu.VMEM((2, line, rows, width), bf16),
            pltpu.VMEM((data_axis, rows, width), bf16),
            pltpu.VMEM((data_axis * rows, features), bf16),
            pltpu.VMEM((expert_axis, share, features), f32),
            pltpu.VMEM((line, share, features), bf16),
            pltpu.VMEM((line, share, features), bf16),
            pltpu.VMEM((2, line, share, features), bf16),
            pltpu.VMEM((2, line, share, features), bf16),
            dma((line, 3)),
            dma((expert_axis,)),
            dma((3, 3)),
            dma((3, data_axis)),
            dma((2, line, SUM_PARTS)),
            dma((2, 2, line, SUM_PARTS)),
            dma((3,)),
            dma((data_axis,)),
            dma((2, line, GRAD_PARTS)),
            dma((2, 2, line, GRAD_PARTS)),
        ],
        compiler_params=pltpu.CompilerParams(
            collective_id=0, has_side_effects=True, vmem_limit_bytes=60 * 1024 * 1024
        ),
    )(
        tokens, expert_ids.T, gate_scores.T, jnp.swapaxes(w_gate, 1, 2),
        jnp.swapaxes(w_up, 1, 2), w_down, projector, student, target_mask.reshape(1, -1),
    )


def finish(teacher_out, projector, student, target_mask):
    grad_scale = 1.0 / math.sqrt(teacher_out.shape[0] * lax.axis_size("expert") * lax.axis_size("dp"))
    mask_rows = target_mask.astype(jnp.float32)
    portion = lax.all_gather(teacher_out, "dp", axis=0, tiled=True)
    proj_part = jnp.dot(portion, projector, preferred_element_type=jnp.float32)
    target_part = student.astype(jnp.float32)
    error_part = (mask_rows[:, None] * (proj_part - target_part)).astype(jnp.bfloat16)
    grad_term = lax.dot_general(
        portion, error_part, (((0,), (0,)), ((), ())), preferred_element_type=jnp.float32
    )
    grad_part = (
        lax.psum_scatter(
            grad_term.astype(jnp.bfloat16), "expert", scatter_dimension=0, tiled=True
        ).astype(jnp.float32)
        * grad_scale
    )
    return (proj_part.astype(jnp.bfloat16), grad_part)


def solution(mesh):
    fits = mesh.shape["expert"] == 8 and mesh.shape["dp"] == 4
    body = fused_body if fits else routed_body
    return jax.shard_map(
        body,
        mesh=mesh,
        in_specs=(
            P(("groups", "expert", "dp"), None),
            P(("groups", "expert", "dp"), None),
            P(("groups", "expert", "dp"), None),
            P(("expert", "dp"), None, None),
            P(("expert", "dp"), None, None),
            P(("expert", "dp"), None, None),
            P(None, "dp"),
            P(("groups", "expert"), "dp"),
            P(("groups", "expert")),
        ),
        out_specs=(P(("groups", "expert"), "dp"), P(("groups", "expert"), "dp")),
        check_vma=False,
    )
```
